512 devices in a mesh: row: 32 (over z, x_hi), col: 16 (over x_lo, y, core).
Axes of the slice: x: 4 (x_hi: 2, x_lo: 2; x = x_hi * 2 + x_lo), y: 4, z: 16, core: 2. Of those that a mesh axis runs over, the one named last changes fastest.
Arguments:
- activations: bfloat16 [1024, 5120], P('row'), may hold values from -6 to 6
- act_basis: bfloat16 [5120, 5120], P('row', 'col'), may hold values from -0.078125 to 0.078125
- gradients: bfloat16 [1024, 27648], P('row', 'col'), may hold values from -6 to 6
- grad_basis: bfloat16 [27648, 27648], P('col', 'row'), may hold values from -0.0390625 to 0.0390625
Outputs:
- correction: float32 [5120, 27648], P('col', 'row')
The draws below stay inside these ranges and needn't reach their ends.
All inputs are finite; a program needn't handle non-finite values.
Results may differ from the reference program's by a relative error of at most 0.0041.
Values may be sent and summed in bfloat16 or wider, within the bound.
No kernel may reach another device: no remote copies, remote signals or barrier semaphores. Data moves between devices by JAX's collectives and lax.ppermute only.
A program may use at most 64 MiB of HBM per device.

```python
import jax
import jax.numpy as jnp
from jax import lax

D = 5120
FF = 27648
SEQ_LEN = 512
SEQS = 2
TOKENS = 1024


def block_scale(stream_key, dims, pieces, smallest, largest):
    level, own = 1.0, jax.random.fold_in(stream_key, 6)
    for dim, shards_of in pieces:
        draws = jnp.exp(jax.random.uniform(jax.random.fold_in(own, dim), (shards_of,), jnp.float32, smallest / len(pieces), largest / len(pieces)))
        level = level * jnp.repeat(draws, dims[dim] // shards_of).reshape([-1 if axis == dim else 1 for axis in range(len(dims))])
    return level


def scatter_about(stream_key, shape, spread, limit, split=(), dtype=jnp.bfloat16):
    array = spread * jax.random.normal(stream_key, shape, jnp.float32)
    if split:
        array = array * block_scale(stream_key, shape, split, -0.22, 0.18)
    return jnp.clip(array, -limit, limit).astype(dtype)


def setup_inputs(seed: int = 0) -> dict:
    splits = jax.random.split(jax.random.key(seed), 5)
    activations = scatter_about(splits[0], (TOKENS, D), 1.0, 6.0, ((0, 32),))
    act_basis = scatter_about(splits[1], (D, D), D ** -0.5, 0.078125, ((0, 32), (1, 16)))
    gradients = scatter_about(splits[2], (TOKENS, FF), 1.0, 6.0, ((0, 32), (1, 16)))
    grad_basis = scatter_about(splits[3], (FF, FF), FF ** -0.5, 0.0390625, ((0, 16), (1, 32)))
    return {"activations": activations, "act_basis": act_basis, "gradients": gradients, "grad_basis": grad_basis}


def reference(activations, act_basis, gradients, grad_basis):
    rotated_acts = jnp.dot(activations, act_basis, preferred_element_type=jnp.float32).astype(jnp.bfloat16)
    rotated_grads = jnp.dot(gradients, grad_basis, preferred_element_type=jnp.float32).astype(jnp.bfloat16)
    total = jnp.zeros((D, FF), jnp.float32)
    for seq_index in range(SEQS):
        acts_seq = rotated_acts[seq_index * SEQ_LEN:(seq_index + 1) * SEQ_LEN]
        grads_seq = rotated_grads[seq_index * SEQ_LEN:(seq_index + 1) * SEQ_LEN]
        seq_grad = lax.dot_general(acts_seq, grads_seq, (((0,), (0,)), ((), ())), preferred_element_type=jnp.float32)
        total = total + seq_grad * seq_grad
    return total / (SEQS * SEQ_LEN)
```

```python
import jax
import jax.numpy as jnp
from jax import lax
from jax.sharding import Mesh
from jax.sharding import PartitionSpec as P

SEQ_LEN = 512
SEQS = 2
NZ, NXH, NXL, NY, NCORE = 16, 2, 2, 4, 2
ROW = ("z", "xh")
COL = ("xl", "y", "core")
SWAP = [(0, 1), (1, 0)]
BF, F32 = jnp.bfloat16, jnp.float32

PARITY = [[p + 2 * k for k in range(NZ // 2)] for p in range(2)]
QUADS = [[(2 * k + i) * NXH + h for i in range(2) for h in range(NXH)] for k in range(NZ // 2)]


def dot(a, b):
    return jnp.dot(a, b, preferred_element_type=F32)


def dot_t(a, b):
    return lax.dot_general(a, b, (((0,), (0,)), ((), ())), preferred_element_type=F32)


def total(x):
    out = x[0].astype(F32)
    for i in range(1, x.shape[0]):
        out = out + x[i].astype(F32)
    return out


def rotate_acts(activations, act_basis):
    tokens, width = activations.shape
    block, cols = act_basis.shape
    parts = activations.reshape(tokens, NZ // 2, 4, block).transpose(2, 0, 1, 3)
    parts = parts.reshape(4, tokens, width // 4)
    parts = lax.all_to_all(parts, ROW, 0, 0, axis_index_groups=QUADS)
    basis = lax.all_gather(act_basis, "z", axis=0, tiled=True, axis_index_groups=PARITY)
    partial = dot(parts.reshape(4 * tokens, width // 4), basis)
    partial = jnp.broadcast_to(
        partial.reshape(2, 1, 2 * tokens, cols), (2, 2, 2 * tokens, cols)
    ).reshape(4, 2 * tokens, cols)
    partial = lax.all_to_all(partial, ROW, 0, 0, axis_index_groups=QUADS)
    rotated = total(partial).astype(BF)
    return lax.all_gather(rotated, "z", axis=0, tiled=True)


def local(activations, act_basis, gradients, grad_basis):
    core = lax.axis_index("core")
    xh = lax.axis_index("xh")
    other = lax.ppermute(gradients, "xh", SWAP)
    pair = jnp.where(
        xh == 0,
        jnp.concatenate([gradients, other]),
        jnp.concatenate([other, gradients]),
    )
    grads = lax.all_gather(pair, "z", axis=0, tiled=True)
    rotated_acts = rotate_acts(activations, act_basis)
    grads, rotated_acts = lax.optimization_barrier((grads, rotated_acts))

    def half(x, index):
        return lax.dynamic_slice_in_dim(x, index * SEQ_LEN, SEQ_LEN, 0)

    theirs = lax.ppermute(dot(half(grads, 1 - core), grad_basis), "core", SWAP)
    partial = (dot(half(grads, core), grad_basis) + theirs).astype(BF)
    n = NXL * NY
    cols = partial.shape[1]
    partial = lax.all_to_all(partial.reshape(n, SEQ_LEN // n, cols), ("xl", "y"), 0, 0)
    own = total(partial).astype(BF)
    own = lax.all_to_all(jnp.broadcast_to(own[None], (n,) + own.shape), ("xl", "y"), 0, 0)
    own = own.reshape(SEQ_LEN, cols)
    rest = lax.ppermute(own, "core", SWAP)
    first = dot_t(half(rotated_acts, core), own)
    second = dot_t(half(rotated_acts, 1 - core), rest)
    return (first * first + second * second) / (SEQS * SEQ_LEN)


def solution(mesh):
    split = Mesh(
        mesh.devices.reshape(NZ, NXH, NXL, NY, NCORE), ("z", "xh", "xl", "y", "core")
    )
    return jax.shard_map(
        local,
        mesh=split,
        in_specs=(P(ROW, None), P(ROW, COL), P(ROW, COL), P(COL, ROW)),
        out_specs=P(COL, ROW),
        check_vma=False,
    )
```

```python
import jax
import jax.numpy as jnp
from jax import lax
from jax.sharding import Mesh
from jax.sharding import PartitionSpec as P

SEQ_LEN = 512
SEQS = 2
NZ, NXH, NXL, NY, NCORE = 16, 2, 2, 4, 2
ROW = ("z", "xh")
COL = ("xl", "y", "core")
SWAP = [(0, 1), (1, 0)]
BF, F32 = jnp.bfloat16, jnp.float32
SPLIT = 896

def dot(a, b):
    return jnp.dot(a, b, preferred_element_type=F32)


def dot_t(a, b):
    return lax.dot_general(a, b, (((0,), (0,)), ((), ())), preferred_element_type=F32)


def total(x):
    out = x[0].astype(F32)
    for i in range(1, x.shape[0]):
        out = out + x[i].astype(F32)
    return out


def tie(*values):
    return lax.optimization_barrier(values)


def spread(x, axes, n):
    return lax.all_to_all(jnp.broadcast_to(x[None], (n,) + x.shape), axes, 0, 0)


def local(activations, act_basis, gradients, grad_basis):
    core = lax.axis_index("core")
    xh = lax.axis_index("xh")
    tokens, width = activations.shape
    cols = grad_basis.shape[1]
    n = NXL * NY

    def swap(x):
        return lax.ppermute(x, "xh", SWAP)

    def in_order(mine, other):
        return jnp.where(xh == 0, mine, other), jnp.where(xh == 0, other, mine)

    hidden, block = gradients.shape[1], act_basis.shape[0]
    pieces = [act_basis[i : i + tokens] for i in range(0, block, tokens)]
    count, act_cols = len(pieces), act_basis.shape[1]
    shared = lax.all_gather(jnp.concatenate([gradients] + pieces, axis=1), "z", axis=0, tiled=True)

    parts = activations.reshape(tokens, NZ, NXH, count, tokens).transpose(2, 3, 0, 1, 4)
    parts = parts.reshape(NXH, count, tokens, NZ * tokens)
    mine, other = in_order(parts[0], parts[1])
    parts = jnp.concatenate([mine, swap(other)], axis=1)
    grad_basis, parts = tie(grad_basis, parts)
    basis_other = swap(grad_basis)

    acts = sum(
        dot(parts[i], shared[:, hidden + i * act_cols : hidden + (i + 1) * act_cols])
        for i in range(count)
    )
    acts_swapped = swap(acts[tokens:])

    half = tokens * NZ // SEQS

    def partial(seq):
        rows = [
            lax.dynamic_slice(shared, (seq * half, lo), (half, hi - lo))
            for lo, hi in ((0, SPLIT), (SPLIT, hidden))
        ]
        return [
            dot(rows[0], b[:SPLIT]) + dot(rows[1], b[SPLIT:]) for b in (grad_basis, basis_other)
        ]

    sums = [
        (a + lax.ppermute(b, "core", SWAP)).astype(BF)
        for a, b in zip(partial(core), partial(1 - core))
    ]
    sums = jnp.stack(in_order(*sums)).reshape(NXH * n, half // n, cols)
    acts, acts_swapped, sums = tie(acts, acts_swapped, sums)
    sums = lax.all_to_all(sums, ("xh", "xl", "y"), 0, 0)
    acts = (acts[:tokens] + acts_swapped).astype(BF)
    acts = lax.all_gather(acts, "z")
    acts, sums = tie(acts, sums)
    acts = jnp.stack(in_order(acts, swap(acts)), axis=1).reshape(SEQS * SEQ_LEN, act_cols)

    sums = sums.reshape(NXH, n, half // n, cols)
    own = jnp.stack([total(sums[h]).astype(BF) for h in range(NXH)])
    own = spread(own, ("xl", "y"), n).reshape(SEQ_LEN, cols)
    rest = lax.ppermute(own, "core", SWAP)

    def seq_grad(seq, g):
        return dot_t(lax.dynamic_slice_in_dim(acts, seq * SEQ_LEN, SEQ_LEN, 0), g)

    first, second = seq_grad(core, own), seq_grad(1 - core, rest)
    return (first * first + second * second) / (SEQS * SEQ_LEN)


def solution(mesh):
    split = Mesh(
        mesh.devices.reshape(NZ, NXH, NXL, NY, NCORE), ("z", "xh", "xl", "y", "core")
    )
    return jax.shard_map(
        local,
        mesh=split,
        in_specs=(P(ROW, None), P(ROW, COL), P(ROW, COL), P(COL, ROW)),
        out_specs=P(COL, ROW),
        check_vma=False,
    )
```

```python
import jax
import jax.numpy as jnp
from jax import lax
from jax.sharding import Mesh
from jax.sharding import PartitionSpec as P

SEQ_LEN = 512
SEQS = 2
NZ, NXH, NXL, NY, NCORE = 16, 2, 2, 4, 2
ROW = ("z", "xh")
COL = ("xl", "y", "core")
SWAP = [(0, 1), (1, 0)]
BF, F32 = jnp.bfloat16, jnp.float32
SPLIT = 1024

PARITY = [[p + 2 * k for k in range(NZ // 2)] for p in range(2)]
QUADS = [[(2 * k + i) * NXH + h for i in range(2) for h in range(NXH)] for k in range(NZ // 2)]

def dot(a, b):
    return jnp.dot(a, b, preferred_element_type=F32)


def dot_t(a, b):
    return lax.dot_general(a, b, (((0,), (0,)), ((), ())), preferred_element_type=F32)


def total(x):
    out = x[0].astype(F32)
    for i in range(1, x.shape[0]):
        out = out + x[i].astype(F32)
    return out


def tie(*values):
    return lax.optimization_barrier(values)


def spread(x, axes, n):
    return lax.all_to_all(jnp.broadcast_to(x[None], (n,) + x.shape), axes, 0, 0)


def local(activations, act_basis, gradients, grad_basis):
    core = lax.axis_index("core")
    xh = lax.axis_index("xh")
    tokens, width = activations.shape
    cols = grad_basis.shape[1]
    n = NXL * NY

    def swap(x):
        return lax.ppermute(x, "xh", SWAP)

    def in_order(mine, other):
        return jnp.where(xh == 0, mine, other), jnp.where(xh == 0, other, mine)

    grads = lax.all_gather(gradients, "z", axis=0, tiled=True)

    block, act_cols = act_basis.shape
    parts = activations.reshape(tokens, NZ // 2, 4, block).transpose(2, 0, 1, 3)
    parts = parts.reshape(4, tokens, width // 4)
    parts = lax.all_to_all(parts, ROW, 0, 0, axis_index_groups=QUADS)
    first, second = grad_basis[:SPLIT], grad_basis[SPLIT:]
    first_other = swap(first)
    rows = lax.all_gather(act_basis, "z", axis=0, tiled=True, axis_index_groups=PARITY)
    acts = dot(parts.reshape(4 * tokens, width // 4), rows).reshape(4, tokens, act_cols)
    acts, first_other = tie(acts, first_other)
    second, acts = tie(second, acts)
    acts = lax.all_to_all(acts, ROW, 0, 0, axis_index_groups=QUADS)
    second_other = swap(second)
    acts = total(acts).astype(BF)
    seq, acts = tie(core, acts)
    acts = spread(acts, "z", NZ)

    half, hidden = tokens * NZ // SEQS, gradients.shape[1]

    def part(seq, lo, hi, basis):
        return dot(lax.dynamic_slice(grads, (seq * half, lo), (half, hi - lo)), basis)

    def products(seq, first, second):
        theirs = part(1 - seq, 0, SPLIT, first) + part(1 - seq, SPLIT, hidden, second)
        theirs = lax.ppermute(theirs, "core", SWAP)
        return (part(seq, 0, SPLIT, first) + part(seq, SPLIT, hidden, second) + theirs).astype(BF)

    sums = products(seq, first, second)
    second_other, sums, acts = tie(second_other, sums, acts)
    sums = in_order(sums, products(seq, first_other, second_other))
    sums = jnp.stack(sums).reshape(NXH * n, half // n, cols)
    sums = lax.all_to_all(sums, ("xh", "xl", "y"), 0, 0)
    acts = jnp.stack(in_order(acts, swap(acts)), axis=1).reshape(SEQS * SEQ_LEN, act_cols)

    sums = sums.reshape(NXH, n, half // n, cols)
    own = jnp.stack([total(sums[h]).astype(BF) for h in range(NXH)])
    own = spread(own, ("xl", "y"), n).reshape(SEQ_LEN, cols)
    rest = lax.ppermute(own, "core", SWAP)

    def seq_grad(seq, g):
        return dot_t(lax.dynamic_slice_in_dim(acts, seq * SEQ_LEN, SEQ_LEN, 0), g)

    first, second = seq_grad(core, own), seq_grad(1 - core, rest)
    return (first * first + second * second) / (SEQS * SEQ_LEN)


def solution(mesh):
    split = Mesh(
        mesh.devices.reshape(NZ, NXH, NXL, NY, NCORE), ("z", "xh", "xl", "y", "core")
    )
    return jax.shard_map(
        local,
        mesh=split,
        in_specs=(P(ROW, None), P(ROW, COL), P(ROW, COL), P(COL, ROW)),
        out_specs=P(COL, ROW),
        check_vma=False,
    )
```

```python
import jax
import jax.numpy as jnp
from jax import lax
from jax.sharding import Mesh
from jax.sharding import PartitionSpec as P

SEQ_LEN = 512
SEQS = 2
NZ, NXH, NXL, NY, NCORE = 16, 2, 2, 4, 2
ROW = ("z", "xh")
COL = ("xl", "y", "core")
SWAP = [(0, 1), (1, 0)]
BF, F32 = jnp.bfloat16, jnp.float32
SPLIT = 1024

PARITY = [[p + 2 * k for k in range(NZ // 2)] for p in range(2)]
QUADS = [[(2 * k + i) * NXH + h for i in range(2) for h in range(NXH)] for k in range(NZ // 2)]

def dot(a, b):
    return jnp.dot(a, b, preferred_element_type=F32)


def dot_t(a, b):
    return lax.dot_general(a, b, (((0,), (0,)), ((), ())), preferred_element_type=F32)


def total(x):
    out = x[0].astype(F32)
    for i in range(1, x.shape[0]):
        out = out + x[i].astype(F32)
    return out


def tie(*values):
    return lax.optimization_barrier(values)


def spread(x, axes, n):
    return lax.all_to_all(jnp.broadcast_to(x[None], (n,) + x.shape), axes, 0, 0)


def local(activations, act_basis, gradients, grad_basis):
    core = lax.axis_index("core")
    xh = lax.axis_index("xh")
    tokens, width = activations.shape
    cols = grad_basis.shape[1]
    n = NXL * NY

    def swap(x):
        return lax.ppermute(x, "xh", SWAP)

    def in_order(mine, other):
        return jnp.where(xh == 0, mine, other), jnp.where(xh == 0, other, mine)

    grads = lax.all_gather(gradients, "z", axis=0, tiled=True)

    block, act_cols = act_basis.shape
    parts = activations.reshape(tokens, NZ // 2, 4, block).transpose(2, 0, 1, 3)
    parts = parts.reshape(4, tokens, width // 4)
    parts = lax.all_to_all(parts, ROW, 0, 0, axis_index_groups=QUADS)
    first, second = grad_basis[:SPLIT], grad_basis[SPLIT:]
    first_other = swap(first)
    rows = lax.all_gather(act_basis, "z", axis=0, tiled=True, axis_index_groups=PARITY)
    acts = dot(parts.reshape(4 * tokens, width // 4), rows).reshape(4, tokens, act_cols)
    acts, first_other = tie(acts, first_other)
    second, acts = tie(second, acts)
    acts = lax.all_to_all(acts, ROW, 0, 0, axis_index_groups=QUADS)
    second_other = swap(second)
    acts = total(acts).astype(BF)
    seq, acts = tie(core, acts)
    acts = spread(acts, "z", NZ)

    half, hidden = tokens * NZ // SEQS, gradients.shape[1]

    def rows_of(seq):
        return [
            lax.dynamic_slice(grads, (seq * half, lo), (half, hi - lo))
            for lo, hi in ((0, SPLIT), (SPLIT, hidden))
        ]

    mine, theirs = tie(rows_of(seq), rows_of(1 - seq))

    def products(first, second):
        added = lax.ppermute(dot(theirs[0], first) + dot(theirs[1], second), "core", SWAP)
        return (dot(mine[0], first) + dot(mine[1], second) + added).astype(BF)

    sums = products(first, second)
    second_other, sums, acts = tie(second_other, sums, acts)
    sums = in_order(sums, products(first_other, second_other))
    sums = jnp.stack(sums).reshape(NXH * n, half // n, cols)
    sums = lax.all_to_all(sums, ("xh", "xl", "y"), 0, 0)
    acts = jnp.stack(in_order(acts, swap(acts)), axis=1).reshape(SEQS * SEQ_LEN, act_cols)

    sums = sums.reshape(NXH, n, half // n, cols)
    own = jnp.stack([total(sums[h]).astype(BF) for h in range(NXH)])
    own = spread(own, ("xl", "y"), n).reshape(SEQ_LEN, cols)
    rest = lax.ppermute(own, "core", SWAP)

    def seq_grad(seq, g):
        return dot_t(lax.dynamic_slice_in_dim(acts, seq * SEQ_LEN, SEQ_LEN, 0), g)

    first, second = seq_grad(core, own), seq_grad(1 - core, rest)
    return (first * first + second * second) / (SEQS * SEQ_LEN)


def solution(mesh):
    split = Mesh(
        mesh.devices.reshape(NZ, NXH, NXL, NY, NCORE), ("z", "xh", "xl", "y", "core")
    )
    return jax.shard_map(
        local,
        mesh=split,
        in_specs=(P(ROW, None), P(ROW, COL), P(ROW, COL), P(COL, ROW)),
        out_specs=P(COL, ROW),
        check_vma=False,
    )
```

```python
import jax
import jax.numpy as jnp
from jax import lax
from jax.sharding import Mesh
from jax.sharding import PartitionSpec as P

SEQ_LEN = 512
SEQS = 2
NZ, NXH, NXL, NY, NCORE = 16, 2, 2, 4, 2
ROW = ("z", "xh")
COL = ("xl", "y", "core")
SWAP = [(0, 1), (1, 0)]
BF, F32 = jnp.bfloat16, jnp.float32
SPLIT = 944

PARITY = [[p + 2 * k for k in range(NZ // 2)] for p in range(2)]
QUADS = [[(2 * k + i) * NXH + h for i in range(2) for h in range(NXH)] for k in range(NZ // 2)]

def dot(a, b):
    return jnp.dot(a, b, preferred_element_type=F32)


def dot_t(a, b):
    return lax.dot_general(a, b, (((0,), (0,)), ((), ())), preferred_element_type=F32)


def total(x):
    out = x[0].astype(F32)
    for i in range(1, x.shape[0]):
        out = out + x[i].astype(F32)
    return out


def tie(*values):
    return lax.optimization_barrier(values)


def spread(x, axes, n):
    return lax.all_to_all(jnp.broadcast_to(x[None], (n,) + x.shape), axes, 0, 0)


def local(activations, act_basis, gradients, grad_basis):
    core = lax.axis_index("core")
    xh = lax.axis_index("xh")
    tokens, width = activations.shape
    cols = grad_basis.shape[1]
    n = NXL * NY

    def swap(x):
        return lax.ppermute(x, "xh", SWAP)

    def in_order(mine, other):
        return jnp.where(xh == 0, mine, other), jnp.where(xh == 0, other, mine)

    grads = lax.all_gather(gradients, "z", axis=0, tiled=True)

    block, act_cols = act_basis.shape
    parts = activations.reshape(tokens, NZ // 2, 4, block).transpose(2, 0, 1, 3)
    parts = parts.reshape(4, tokens, width // 4)
    parts = lax.all_to_all(parts, ROW, 0, 0, axis_index_groups=QUADS)
    first, second = grad_basis[:SPLIT], grad_basis[SPLIT:]
    first_other = swap(first)
    rows = lax.all_gather(act_basis, "z", axis=0, tiled=True, axis_index_groups=PARITY)
    acts = dot(parts.reshape(4 * tokens, width // 4), rows).reshape(4, tokens, act_cols)
    acts, first_other = tie(acts, first_other)
    second, acts = tie(second, acts)
    acts = lax.all_to_all(acts, ROW, 0, 0, axis_index_groups=QUADS)
    second_other = swap(second)
    acts = total(acts).astype(BF)
    seq, acts = tie(core, acts)
    acts = spread(acts, "z", NZ)

    half, hidden = tokens * NZ // SEQS, gradients.shape[1]

    def rows_of(seq):
        return [
            lax.dynamic_slice(grads, (seq * half, lo), (half, hi - lo))
            for lo, hi in ((0, SPLIT), (SPLIT, hidden))
        ]

    mine, theirs = tie(rows_of(seq), rows_of(1 - seq))

    def rounded(second, started):
        theirs_first, mine_first = started
        added = lax.ppermute(theirs_first + dot(theirs[1], second), "core", SWAP)
        return (mine_first + dot(mine[1], second) + added).astype(BF)

    def start(first):
        return dot(theirs[0], first), dot(mine[0], first)

    sums = rounded(second, start(first))
    second_other, sums, acts, started = tie(second_other, sums, acts, start(first_other))
    sums = in_order(sums, rounded(second_other, started))
    sums = jnp.stack(sums).reshape(NXH * n, half // n, cols)
    sums = lax.all_to_all(sums, ("xh", "xl", "y"), 0, 0)
    acts = jnp.stack(in_order(acts, swap(acts)), axis=1).reshape(SEQS * SEQ_LEN, act_cols)

    sums = sums.reshape(NXH, n, half // n, cols)
    own = jnp.stack([total(sums[h]).astype(BF) for h in range(NXH)])
    own = spread(own, ("xl", "y"), n).reshape(SEQ_LEN, cols)
    rest = lax.ppermute(own, "core", SWAP)

    def seq_grad(seq, g):
        return dot_t(lax.dynamic_slice_in_dim(acts, seq * SEQ_LEN, SEQ_LEN, 0), g)

    first, second = seq_grad(core, own), seq_grad(1 - core, rest)
    return (first * first + second * second) / (SEQS * SEQ_LEN)


def solution(mesh):
    split = Mesh(
        mesh.devices.reshape(NZ, NXH, NXL, NY, NCORE), ("z", "xh", "xl", "y", "core")
    )
    return jax.shard_map(
        local,
        mesh=split,
        in_specs=(P(ROW, None), P(ROW, COL), P(ROW, COL), P(COL, ROW)),
        out_specs=P(COL, ROW),
        check_vma=False,
    )
```

```python
import jax
import jax.numpy as jnp
from jax import lax
from jax.sharding import Mesh
from jax.sharding import PartitionSpec as P

SEQ_LEN = 512
SEQS = 2
NZ, NXH, NXL, NY, NCORE = 16, 2, 2, 4, 2
ROW = ("z", "xh")
COL = ("xl", "y", "core")
SWAP = [(0, 1), (1, 0)]
BF, F32 = jnp.bfloat16, jnp.float32
SPLIT = 944

PARITY = [[p + 2 * k for k in range(NZ // 2)] for p in range(2)]
QUADS = [[(2 * k + i) * NXH + h for i in range(2) for h in range(NXH)] for k in range(NZ // 2)]

def dot(a, b):
    return jnp.dot(a, b, preferred_element_type=F32)


def dot_t(a, b):
    return lax.dot_general(a, b, (((0,), (0,)), ((), ())), preferred_element_type=F32)


def total(x):
    out = x[0].astype(F32)
    for i in range(1, x.shape[0]):
        out = out + x[i].astype(F32)
    return out


def tie(*values):
    return lax.optimization_barrier(values)


def spread(x, axes, n):
    return lax.all_to_all(jnp.broadcast_to(x[None], (n,) + x.shape), axes, 0, 0)


def local(activations, act_basis, gradients, grad_basis):
    core = lax.axis_index("core")
    xh = lax.axis_index("xh")
    tokens, width = activations.shape
    cols = grad_basis.shape[1]
    n = NXL * NY

    def swap(x):
        return lax.ppermute(x, "xh", SWAP)

    def in_order(mine, other):
        return jnp.where(xh == 0, mine, other), jnp.where(xh == 0, other, mine)

    grads = lax.all_gather(gradients, "z", axis=0, tiled=True)

    block, act_cols = act_basis.shape
    parts = activations.reshape(tokens, NZ // 2, 4, block).transpose(2, 0, 1, 3)
    parts = parts.reshape(4, tokens, width // 4)
    parts = lax.all_to_all(parts, ROW, 0, 0, axis_index_groups=QUADS)
    first, second = grad_basis[:SPLIT], grad_basis[SPLIT:]
    first_other = swap(first)
    rows = lax.all_gather(act_basis, "z", axis=0, tiled=True, axis_index_groups=PARITY)
    acts = dot(parts.reshape(4 * tokens, width // 4), rows).reshape(4, tokens, act_cols)
    acts, first_other = tie(acts, first_other)
    second, acts = tie(second, acts)
    acts = lax.all_to_all(acts, ROW, 0, 0, axis_index_groups=QUADS)
    second_other = swap(second)
    acts = total(acts).astype(BF)
    seq, acts = tie(core, acts)
    acts = jnp.concatenate([acts[: tokens // 2], acts[tokens // 2 :]], axis=1)
    acts = spread(acts, "z", NZ)

    half, hidden = tokens * NZ // SEQS, gradients.shape[1]

    def rows_of(seq):
        return [
            lax.dynamic_slice(grads, (seq * half, lo), (half, hi - lo))
            for lo, hi in ((0, SPLIT), (SPLIT, hidden))
        ]

    mine, theirs = tie(rows_of(seq), rows_of(1 - seq))

    def rounded(second, started):
        theirs_first, mine_first = started
        added = lax.ppermute(theirs_first + dot(theirs[1], second), "core", SWAP)
        return (mine_first + dot(mine[1], second) + added).astype(BF)

    def start(first):
        return dot(theirs[0], first), dot(mine[0], first)

    sums = rounded(second, start(first))
    second_other, sums, acts, started = tie(second_other, sums, acts, start(first_other))
    sums = in_order(sums, rounded(second_other, started))
    sums = jnp.stack(sums).reshape(NXH * n, half // n, cols)
    sums = lax.all_to_all(sums, ("xh", "xl", "y"), 0, 0)
    acts = jnp.stack(in_order(acts, swap(acts)), axis=1)
    acts = jnp.concatenate([acts[..., :act_cols], acts[..., act_cols:]], axis=2)
    acts = acts.reshape(SEQS * SEQ_LEN, act_cols)

    sums = sums.reshape(NXH, n, half // n, cols)
    own = jnp.stack([total(sums[h]).astype(BF) for h in range(NXH)])
    own = spread(own, ("xl", "y"), n).reshape(SEQ_LEN, cols)
    rest = lax.ppermute(own, "core", SWAP)

    def seq_grad(seq, g):
        return dot_t(lax.dynamic_slice_in_dim(acts, seq * SEQ_LEN, SEQ_LEN, 0), g)

    first, second = seq_grad(core, own), seq_grad(1 - core, rest)
    return (first * first + second * second) / (SEQS * SEQ_LEN)


def solution(mesh):
    split = Mesh(
        mesh.devices.reshape(NZ, NXH, NXL, NY, NCORE), ("z", "xh", "xl", "y", "core")
    )
    return jax.shard_map(
        local,
        mesh=split,
        in_specs=(P(ROW, None), P(ROW, COL), P(ROW, COL), P(COL, ROW)),
        out_specs=P(COL, ROW),
        check_vma=False,
    )
```
